32 devices in a mesh: month: 4 (over y, x), grid: 8 (over z, core).
Axes of the slice: x: 2, y: 2, z: 4, core: 2. Of those that a mesh axis runs over, the one named last changes fastest.
Arguments:
- tracers: float32 [64, 8192], P(None, 'grid'), may hold values from 0.25 to 7
- targets: float32 [64], replicated, may hold values from 0.5 to 2
- retain: float32 [8, 8192], P('month', 'grid'), may hold values from 0.5 to 0.95
- blocks: float32 [8, 64, 8, 128, 128], P('month', 'grid'), may hold values from 3.90625e-07 to 0.00390625
- cols: int32 [8, 64, 8], P('month', 'grid'), may hold values from 0 to 63, as said below
Outputs:
- spun_up: float32 [64, 8192], P('month', 'grid')
The draws below stay inside these ranges and needn't reach their ends.
Inputs may be any that keep to these rules, and one draw needn't show every extreme that they name: cols[m, i, 0] = i; for 1 <= k < 6, cols[m, i, k] names a block on the same grid device as block i (block b lies on device b // 8); the last 2 entries name blocks on other devices, and of the 16 such entries of one device's block rows in one month at most 3 lie on any single device, exactly 3 on some.
All inputs are finite; a program needn't handle non-finite values.
Results may differ from the reference program's by a relative error of at most 0.0001.
Values sent between devices are 32-bit elements; how exact they have to be, the bound alone decides.
A program may use at most 64 MiB of HBM per device.

```python
import math
import jax
import jax.numpy as jnp
from jax import lax

BS = 128
NB_DEV = 8
K = 8
KF = 2
MONTHS = 8
TRACERS = 64
NBLK = 64
NPTS = 8192
CAP = 3
N_GRID = 8


def draw_tracers(key, part):
    ramp_pos = jnp.arange(NPTS, dtype=jnp.float32) / NPTS
    base = jax.random.uniform(key, (TRACERS, NPTS), jnp.float32, 0.5, 1.5)
    ramp = 1.0 + 2.0 * ramp_pos
    return (base * ramp[None, :]).astype(jnp.float32)


def device_cols(dev_key, owner):
    keys = jax.random.split(dev_key, 5)
    far_count = NB_DEV * KF
    slots_all = CAP * (N_GRID - 1)
    diag_col = owner * NB_DEV + jnp.arange(NB_DEV, dtype=jnp.int32)
    near = jax.random.randint(keys[0], (NB_DEV, K - KF - 1), 0, NB_DEV).astype(jnp.int32) + owner * NB_DEV
    rest = jax.random.permutation(keys[1], slots_all - CAP).astype(jnp.int32) + CAP
    values = jnp.concatenate([jnp.arange(CAP, dtype=jnp.int32), rest[:far_count - CAP]])
    values = values[jax.random.permutation(keys[2], far_count)]
    peer_map = jax.random.permutation(keys[3], N_GRID - 1).astype(jnp.int32)
    peer = (owner + 1 + peer_map[values // CAP]) % N_GRID
    inner = jax.random.randint(keys[4], (far_count,), 0, NB_DEV).astype(jnp.int32)
    far = (peer * NB_DEV + inner).reshape(NB_DEV, KF)
    return jnp.concatenate([diag_col[:, None], near, far], axis=1)


def draw_cols(key, part):
    own_key = jax.random.fold_in(key, 7)
    keys = jax.random.split(own_key, MONTHS * N_GRID)
    owners = (jnp.arange(MONTHS * N_GRID, dtype=jnp.int32) % N_GRID).astype(jnp.int32)
    table = jax.vmap(device_cols)(keys, owners)
    return table.reshape(MONTHS, NBLK, K).astype(jnp.int32)


def level_of(key, shape, shards, low, top_value):
    gain = 1.0
    for dim, blocks in shards:
        heights = jax.random.uniform(jax.random.fold_in(jax.random.fold_in(key, 6), dim), (blocks,), jnp.float32, low / len(shards), top_value / len(shards))
        gain = gain * jnp.repeat(jnp.exp(heights), shape[dim] // blocks).reshape((-1,) + (1,) * (len(shape) - 1 - dim))
    return gain


def setup_inputs(seed: int = 0) -> dict:
    splits = jax.random.split(jax.random.key(seed), 6)
    tracers = draw_tracers(jax.random.fold_in(splits[5], 71), 0)
    targets = jnp.clip(jnp.exp(jax.random.uniform(splits[1], (TRACERS,), jnp.float32, math.log(0.5), math.log(2.0))), 0.5, 2.0)
    retain = jnp.clip(jnp.exp(math.log(0.95) - 0.64185387 * jax.random.uniform(splits[2], (MONTHS, NPTS), jnp.float32) ** level_of(splits[2], (MONTHS, NPTS), ((0, 4), (1, 8)), -0.2, 0.2)), 0.5, 0.95)
    blocks = jnp.clip(jnp.exp(math.log(0.00390625) - 9.2103404 * jax.random.uniform(splits[3], (MONTHS, NBLK, K, BS, BS), jnp.float32) ** level_of(splits[3], (MONTHS, NBLK, K, BS, BS), ((0, 4), (1, 8)), -0.2, 0.2)), 3.906249901319825e-07, 0.00390625)
    cols = draw_cols(jax.random.fold_in(splits[5], 71), 0)
    return dict(tracers=tracers, targets=targets, retain=retain, blocks=blocks, cols=cols)


def reference(tracers, targets, retain, blocks, cols):
    state = tracers
    for month_idx in range(MONTHS):
        view = state.reshape(TRACERS, NBLK, BS)
        picked = view[:, cols[month_idx]]
        mixed = jnp.einsum("tbkc,bkrc->tbr", picked, blocks[month_idx], precision=lax.Precision.HIGHEST, preferred_element_type=jnp.float32)
        state = retain[month_idx][None, :] * state + mixed.reshape(TRACERS, NPTS)
    inventory = jnp.sum(state, axis=1)
    return state * (targets * NPTS / inventory)[:, None]
```

```python
import functools

import jax
import jax.numpy as jnp
from jax import lax
from jax.experimental import pallas as pl
from jax.experimental.pallas import tpu as pltpu
from jax.sharding import PartitionSpec as P

FAR = 2
TB = 8
NT = (((1,), (1,)), ((), ()))
F32, BF16, I32 = jnp.float32, jnp.bfloat16, jnp.int32


def kernel(
    sections, n, cap, months, nb, kk, bs, nbatch,
    tracers, targets, retain, blocks, cols_s, cols_v,
    out,
    wf, whi, wlo, xin, xmid, xout, hl, cur, far, acc, sendbuf, recv, psend, precv, fout,
    cstage, crecv, csmem, send_tab, pos_tab,
    w_sem, c_send, c_recv, c_loc, h_send, h_recv, in_send, in_recv, p_send, p_recv, o_send, o_recv,
):
    tb = TB
    near = kk - FAR
    per = nbatch // sections
    last = sections - 1
    nfar = nb * FAR
    npts = float(n * nb * bs)
    s = lax.axis_index("month")
    g = lax.axis_index("grid")
    offsets = sorted(range(1, n), key=lambda o: abs(o - n // 2))

    def peer(o):
        return lax.rem(g + o, n)

    def chunk(j, i):
        return pltpu.make_async_copy(blocks.at[j, i], wf.at[j, i], w_sem.at[j, i])

    for j in range(months):
        for i in range(nb):
            chunk(j, i).start()

    barrier = pltpu.get_barrier_semaphore()
    for o in range(1, n):
        pl.semaphore_signal(barrier, inc=1, device_id={"grid": peer(o)}, device_id_type=pl.DeviceIdType.MESH)
    for o in range(1, sections):
        pl.semaphore_signal(
            barrier, inc=1, device_id={"month": lax.rem(s + o, sections)}, device_id_type=pl.DeviceIdType.MESH
        )
    cstage[...] = jnp.broadcast_to(cols_v[...], cstage.shape)
    pl.semaphore_wait(barrier, n - 1 + sections - 1)

    for o in offsets:
        pltpu.make_async_remote_copy(
            cstage, crecv.at[o - 1], c_send, c_recv,
            device_id={"grid": peer(o)}, device_id_type=pl.DeviceIdType.MESH,
        ).start()

    @pl.when(s == 0)
    def _():
        for b in range(nbatch):
            for i in range(nb):
                xin[b, i] = tracers[b * tb : (b + 1) * tb, i * bs : (i + 1) * bs]

    def far_at(j, e):
        return j * nb * kk + (e // FAR) * kk + near + e % FAR

    for j in range(months):
        owners = [cols_s[0, far_at(j, e)] // nb for e in range(nfar)]
        for e in range(nfar):
            rank = I32(0)
            for f in range(e):
                rank = rank + jnp.where(owners[f] == owners[e], 1, 0)
            off = g - owners[e]
            off = jnp.where(off < 0, off + n, off)
            pos_tab[j * nfar + e] = jnp.clip((off - 1) * cap + rank, 0, (n - 1) * cap - 1)

    pltpu.make_async_copy(crecv, crecv, c_recv).wait()
    local = pltpu.make_async_copy(crecv, csmem, c_loc)
    local.start()
    local.wait()

    def make_table(j):
        def one(q, carry):
            o = q + 1
            count = I32(0)
            idx = [I32(0)] * cap
            for e in range(nfar):
                c = csmem[n - 1 - o, 0, far_at(j, e)] - g * nb
                hit = (c >= 0) & (c < nb)
                for r in range(cap):
                    idx[r] = jnp.where(hit & (count == r), c, idx[r])
                count = count + jnp.where(hit, 1, 0)
            for r in range(cap):
                send_tab[(j * (n - 1) + q) * cap + r] = idx[r]
            return carry

        lax.fori_loop(0, n - 1, one, 0)

    def prep(j):
        def one(i, carry):
            chunk(j, i).wait()
            for k in range(kk):
                b = wf[j, i, k]
                hi = b.astype(BF16)
                whi[j, i, :, k * bs : (k + 1) * bs] = hi
                wlo[j, i, :, k * bs : (k + 1) * bs] = (b - hi.astype(F32)).astype(BF16)
            return carry

        lax.fori_loop(0, nb, one, 0)

    def split(v):
        hi = v.astype(BF16).astype(F32)
        return jnp.concatenate([hi, v - hi], axis=0).astype(BF16)

    def product(rows, j, i, lo, hi):
        d = lax.dot_general(rows, whi[j, i, :, lo * bs : hi * bs], NT, preferred_element_type=F32)
        d = d + lax.dot_general(rows, wlo[j, i, :, lo * bs : hi * bs], NT, preferred_element_type=F32)
        return d[:tb] + d[tb:]

    def send_halo(b, j, src):
        for i in range(nb):
            cur[i] = src[b, i]
        for o in offsets:
            for r in range(cap):
                q = (o - 1) * cap + r
                idx = send_tab[j * (n - 1) * cap + q]
                sendbuf[b, j, q] = cur[idx]
            pltpu.make_async_remote_copy(
                sendbuf.at[b, j, pl.ds((o - 1) * cap, cap)],
                recv.at[b, j, pl.ds((o - 1) * cap, cap)],
                h_send.at[b, j], h_recv.at[b, j],
                device_id={"grid": peer(o)}, device_id_type=pl.DeviceIdType.MESH,
            ).start()

    def apply(b, j, src, dst):
        for i in range(nb):
            hl[i] = split(src[b, i])
        for i in range(nb):
            picked = [hl[i]]
            for k in range(1, near):
                picked.append(hl[jnp.clip(cols_s[0, j * nb * kk + i * kk + k] - g * nb, 0, nb - 1)])
            rows = jnp.concatenate(picked, axis=1)
            keep = retain[j : j + 1, i * bs : (i + 1) * bs]
            acc[i] = keep * src[b, i] + product(rows, j, i, 0, near)
        pltpu.make_async_copy(recv.at[b, j], recv.at[b, j], h_recv.at[b, j]).wait()
        for q in range((n - 1) * cap):
            far[q] = split(recv[b, j, q])
        for i in range(nb):
            rows = jnp.concatenate([far[pos_tab[j * nfar + i * FAR + f]] for f in range(FAR)], axis=1)
            dst[b, i] = acc[i] + product(rows, j, i, near, kk)

    def enter(b):
        @pl.when(s > 0)
        def _():
            pltpu.make_async_copy(xin.at[b], xin.at[b], in_recv.at[b]).wait()

        send_halo(b, 0, xin)

    def middle(b):
        apply(b, 0, xin, xmid)
        send_halo(b, 1, xmid)

    def passed(b):
        return pltpu.make_async_remote_copy(
            xout.at[b], xin.at[b], in_send.at[b], in_recv.at[b],
            device_id={"month": lax.rem(s + 1, sections)}, device_id_type=pl.DeviceIdType.MESH,
        )

    def leave(b):
        apply(b, 1, xmid, xout)

        @pl.when(s < last)
        def _():
            passed(b).start()

        @pl.when(s == last)
        def _():
            total = xout[b, 0]
            for i in range(1, nb):
                total = total + xout[b, i]
            psend[b] = jnp.broadcast_to(jnp.sum(total, axis=1, keepdims=True), (tb, bs))
            for o in offsets:
                pltpu.make_async_remote_copy(
                    psend.at[b], precv.at[b, o - 1], p_send.at[b], p_recv.at[b],
                    device_id={"grid": peer(o)}, device_id_type=pl.DeviceIdType.MESH,
                ).start()

    def delivered(b):
        row = pl.multiple_of(lax.rem(b, per) * tb, tb)
        return pltpu.make_async_remote_copy(
            fout.at[b], out.at[pl.ds(row, tb)], o_send.at[b], o_recv,
            device_id={"month": lax.div(b, per)}, device_id_type=pl.DeviceIdType.MESH,
        )

    def finish(b):
        @pl.when(s == last)
        def _():
            pltpu.make_async_copy(precv.at[b], precv.at[b], p_recv.at[b]).wait()
            total = psend[b]
            for o in range(1, n):
                total = total + precv[b, o - 1]
            wide = jnp.broadcast_to(targets[...], (tb, targets.shape[1]))
            row = lax.broadcasted_iota(I32, wide.shape, 0) + b * tb
            col = lax.broadcasted_iota(I32, wide.shape, 1)
            goal = jnp.sum(jnp.where(row == col, wide, 0.0), axis=1, keepdims=True)
            factor = goal * npts / total
            for i in range(nb):
                fout[b, :, i * bs : (i + 1) * bs] = xout[b, i] * factor

            @pl.when(b < last * per)
            def _():
                delivered(b).start()

            @pl.when(b >= last * per)
            def _():
                at = pl.multiple_of(lax.rem(b, per) * tb, tb)
                out[pl.ds(at, tb), :] = fout[b]

    make_table(0)

    @pl.when(s == 0)
    def _():
        enter(I32(0))
        make_table(1)
        prep(0)

    @pl.when(s > 0)
    def _():
        make_table(1)
        prep(0)
        prep(1)
        enter(I32(0))

    middle(I32(0))

    @pl.when(s == 0)
    def _():
        prep(1)

    def step(b, carry):
        enter(b)
        leave(b - 1)
        middle(b)
        finish(b - 1)
        return carry

    lax.fori_loop(1, nbatch, step, 0)
    leave(I32(nbatch - 1))
    finish(I32(nbatch - 1))

    pltpu.make_async_copy(crecv, crecv, c_send).wait()

    def drain(b, carry):
        for j in range(months):
            pltpu.make_async_copy(sendbuf.at[b, j], sendbuf.at[b, j], h_send.at[b, j]).wait()

        @pl.when(s < last)
        def _():
            passed(b).wait_send()

        @pl.when(s == last)
        def _():
            pltpu.make_async_copy(precv.at[b], precv.at[b], p_send.at[b]).wait()

            @pl.when(b < last * per)
            def _():
                delivered(b).wait_send()

        return carry

    lax.fori_loop(0, nbatch, drain, 0)

    @pl.when(s < last)
    def _():
        pltpu.make_async_copy(out, out, o_recv).wait()


def solution(mesh):
    sections, n = mesh.shape["month"], mesh.shape["grid"]

    def local(tracers, targets, retain, blocks, cols):
        months, nb, kk, bs = blocks.shape[:4]
        count, rows = tracers.shape
        nbatch = count // TB
        cap = -(-nb * FAR // (n - 1))
        slots = (n - 1) * cap
        flat = cols.reshape(1, -1)
        dma = pltpu.SemaphoreType.DMA
        vmem = pl.BlockSpec(memory_space=pltpu.VMEM)
        return pl.pallas_call(
            functools.partial(kernel, sections, n, cap, months, nb, kk, bs, nbatch),
            out_shape=jax.ShapeDtypeStruct((count // sections, rows), F32),
            in_specs=[
                vmem, vmem, vmem,
                pl.BlockSpec(memory_space=pl.ANY),
                pl.BlockSpec(memory_space=pltpu.SMEM),
                vmem,
            ],
            out_specs=vmem,
            scratch_shapes=[
                pltpu.VMEM((months, nb, kk, bs, bs), F32),
                pltpu.VMEM((months, nb, bs, kk * bs), BF16),
                pltpu.VMEM((months, nb, bs, kk * bs), BF16),
                pltpu.VMEM((nbatch, nb, TB, bs), F32),
                pltpu.VMEM((nbatch, nb, TB, bs), F32),
                pltpu.VMEM((nbatch, nb, TB, bs), F32),
                pltpu.VMEM((nb, 2 * TB, bs), BF16),
                pltpu.VMEM((nb, TB, bs), F32),
                pltpu.VMEM((slots, 2 * TB, bs), BF16),
                pltpu.VMEM((nb, TB, bs), F32),
                pltpu.VMEM((nbatch, months, slots, TB, bs), F32),
                pltpu.VMEM((nbatch, months, slots, TB, bs), F32),
                pltpu.VMEM((nbatch, TB, bs), F32),
                pltpu.VMEM((nbatch, n - 1, TB, bs), F32),
                pltpu.VMEM((nbatch, TB, rows), F32),
                pltpu.VMEM((8, flat.shape[1]), I32),
                pltpu.VMEM((n - 1, 8, flat.shape[1]), I32),
                pltpu.SMEM((n - 1, 8, flat.shape[1]), I32),
                pltpu.SMEM((months * slots,), I32),
                pltpu.SMEM((months * nb * FAR,), I32),
                dma((months, nb)),
                dma, dma, dma,
                dma((nbatch, months)), dma((nbatch, months)),
                dma((nbatch,)), dma((nbatch,)),
                dma((nbatch,)), dma((nbatch,)),
                dma((nbatch,)), dma,
            ],
            compiler_params=pltpu.CompilerParams(
                collective_id=0, has_side_effects=True, vmem_limit_bytes=48 * 1024 * 1024
            ),
        )(tracers, targets.reshape(1, -1), retain, blocks, flat, flat)

    return jax.shard_map(
        local,
        mesh=mesh,
        in_specs=(
            P(None, "grid"),
            P(),
            P("month", "grid"),
            P("month", "grid", None, None, None),
            P("month", "grid", None),
        ),
        out_specs=P("month", "grid"),
        check_vma=False,
    )
```

```python
import functools

import jax
import jax.numpy as jnp
from jax import lax
from jax.experimental import pallas as pl
from jax.experimental.pallas import tpu as pltpu
from jax.sharding import PartitionSpec as P

FAR = 2
TB = 8
F32, BF16, I32 = jnp.float32, jnp.bfloat16, jnp.int32


def kernel(
    sections, n, cap, months, nb, kk, bs, nbatch,
    tracers_h, targets_h, retain_h, blocks, cols_h,
    out,
    tracers, targets, retain, cols_s,
    wf, whi, wlo, xin, xmid, xout, hl, cur, far, acc, sendbuf, recv, psend, precv, fout,
    crecv, csmem, send_tab, pos_tab,
    a_sem, w_sem, c_send, c_recv, c_loc, h_send, h_recv, in_send, in_recv, p_send, p_recv, o_send, o_recv,
):
    tb = TB
    near = kk - FAR
    per = nbatch // sections
    last = sections - 1
    nfar = nb * FAR
    npts = float(n * nb * bs)
    s = lax.axis_index("month")
    g = lax.axis_index("grid")
    offsets = sorted(range(1, n), key=lambda o: abs(o - n // 2))

    def peer(o):
        return lax.rem(g + o, n)

    def chunk(j, i):
        return pltpu.make_async_copy(blocks.at[j, i], wf.at[j, i], w_sem.at[j, i])

    get_cols = pltpu.make_async_copy(cols_h, cols_s, a_sem.at[0])
    get_tracers = pltpu.make_async_copy(tracers_h, tracers, a_sem.at[1])
    get_retain = pltpu.make_async_copy(retain_h, retain, a_sem.at[2])
    get_targets = pltpu.make_async_copy(targets_h, targets, a_sem.at[3])
    get_cols.start()
    get_tracers.start()
    get_retain.start()
    get_targets.start()
    for j in range(months):
        for i in range(nb):
            chunk(j, i).start()

    barrier = pltpu.get_barrier_semaphore()
    for o in range(1, n):
        pl.semaphore_signal(barrier, inc=1, device_id={"grid": peer(o)}, device_id_type=pl.DeviceIdType.MESH)
    for o in range(1, sections):
        pl.semaphore_signal(
            barrier, inc=1, device_id={"month": lax.rem(s + o, sections)}, device_id_type=pl.DeviceIdType.MESH
        )
    pl.semaphore_wait(barrier, n - 1 + sections - 1)

    for o in offsets:
        pltpu.make_async_remote_copy(
            cols_h, crecv.at[o - 1], c_send, c_recv,
            device_id={"grid": peer(o)}, device_id_type=pl.DeviceIdType.MESH,
        ).start()

    get_cols.wait()
    get_tracers.wait()
    get_retain.wait()
    get_targets.wait()

    @pl.when(s == 0)
    def _():
        for b in range(nbatch):
            for i in range(nb):
                xin[b, i] = tracers[b * tb : (b + 1) * tb, i * bs : (i + 1) * bs]

    def far_at(j, e):
        return j, e // FAR, near + e % FAR

    for j in range(months):
        owners = [cols_s[far_at(j, e)] // nb for e in range(nfar)]
        for e in range(nfar):
            rank = I32(0)
            for f in range(e):
                rank = rank + jnp.where(owners[f] == owners[e], 1, 0)
            off = g - owners[e]
            off = jnp.where(off < 0, off + n, off)
            pos_tab[j * nfar + e] = jnp.clip((off - 1) * cap + rank, 0, (n - 1) * cap - 1)

    pltpu.make_async_copy(crecv, crecv, c_recv).wait()
    local = pltpu.make_async_copy(crecv, csmem, c_loc)
    local.start()
    local.wait()

    def make_table(j):
        def one(q, carry):
            o = q + 1
            count = I32(0)
            idx = [I32(0)] * cap
            for e in range(nfar):
                c = csmem[(n - 1 - o,) + far_at(j, e)] - g * nb
                hit = (c >= 0) & (c < nb)
                for r in range(cap):
                    idx[r] = jnp.where(hit & (count == r), c, idx[r])
                count = count + jnp.where(hit, 1, 0)
            for r in range(cap):
                send_tab[(j * (n - 1) + q) * cap + r] = idx[r]
            return carry

        lax.fori_loop(0, n - 1, one, 0)

    def prep(j):
        def one(i, carry):
            chunk(j, i).wait()
            for k in range(kk):
                b = wf[j, i, k].T
                hi = b.astype(BF16)
                whi[j, i, k * bs : (k + 1) * bs, :] = hi
                wlo[j, i, k * bs : (k + 1) * bs, :] = (b - hi.astype(F32)).astype(BF16)
            return carry

        lax.fori_loop(0, nb, one, 0)

    def split(v):
        hi = v.astype(BF16).astype(F32)
        return jnp.concatenate([hi, v - hi], axis=0).astype(BF16)

    def product(rows, j, i, lo, hi):
        d = jnp.dot(rows, whi[j, i, lo * bs : hi * bs, :], preferred_element_type=F32)
        d = d + jnp.dot(rows, wlo[j, i, lo * bs : hi * bs, :], preferred_element_type=F32)
        return d[:tb] + d[tb:]

    def send_halo(b, j, src):
        for i in range(nb):
            cur[i] = src[b, i]
        for o in offsets:
            for r in range(cap):
                q = (o - 1) * cap + r
                idx = send_tab[j * (n - 1) * cap + q]
                sendbuf[b, j, q] = cur[idx]
            pltpu.make_async_remote_copy(
                sendbuf.at[b, j, pl.ds((o - 1) * cap, cap)],
                recv.at[b, j, pl.ds((o - 1) * cap, cap)],
                h_send.at[b, j], h_recv.at[b, j],
                device_id={"grid": peer(o)}, device_id_type=pl.DeviceIdType.MESH,
            ).start()

    def apply(b, j, src, dst):
        for i in range(nb):
            hl[i] = split(src[b, i])
        for i in range(nb):
            picked = [hl[i]]
            for k in range(1, near):
                picked.append(hl[jnp.clip(cols_s[j, i, k] - g * nb, 0, nb - 1)])
            rows = jnp.concatenate(picked, axis=1)
            keep = retain[j : j + 1, i * bs : (i + 1) * bs]
            acc[i] = keep * src[b, i] + product(rows, j, i, 0, near)
        pltpu.make_async_copy(recv.at[b, j], recv.at[b, j], h_recv.at[b, j]).wait()
        for q in range((n - 1) * cap):
            far[q] = split(recv[b, j, q])
        for i in range(nb):
            rows = jnp.concatenate([far[pos_tab[j * nfar + i * FAR + f]] for f in range(FAR)], axis=1)
            dst[b, i] = acc[i] + product(rows, j, i, near, kk)

    def enter(b):
        @pl.when(s > 0)
        def _():
            pltpu.make_async_copy(xin.at[b], xin.at[b], in_recv.at[b]).wait()

        send_halo(b, 0, xin)

    def middle(b):
        apply(b, 0, xin, xmid)
        send_halo(b, 1, xmid)

    def passed(b):
        return pltpu.make_async_remote_copy(
            xout.at[b], xin.at[b], in_send.at[b], in_recv.at[b],
            device_id={"month": lax.rem(s + 1, sections)}, device_id_type=pl.DeviceIdType.MESH,
        )

    def leave(b):
        apply(b, 1, xmid, xout)

        @pl.when(s < last)
        def _():
            passed(b).start()

        @pl.when(s == last)
        def _():
            total = xout[b, 0]
            for i in range(1, nb):
                total = total + xout[b, i]
            psend[b] = jnp.broadcast_to(jnp.sum(total, axis=1, keepdims=True), (tb, bs))
            for o in offsets:
                pltpu.make_async_remote_copy(
                    psend.at[b], precv.at[b, o - 1], p_send.at[b], p_recv.at[b],
                    device_id={"grid": peer(o)}, device_id_type=pl.DeviceIdType.MESH,
                ).start()

    def delivered(b):
        row = pl.multiple_of(lax.rem(b, per) * tb, tb)
        return pltpu.make_async_remote_copy(
            fout.at[b], out.at[pl.ds(row, tb)], o_send.at[b], o_recv,
            device_id={"month": lax.div(b, per)}, device_id_type=pl.DeviceIdType.MESH,
        )

    def finish(b):
        @pl.when(s == last)
        def _():
            pltpu.make_async_copy(precv.at[b], precv.at[b], p_recv.at[b]).wait()
            total = psend[b]
            for o in range(1, n):
                total = total + precv[b, o - 1]
            wide = jnp.broadcast_to(targets[...], (tb, targets.shape[1]))
            row = lax.broadcasted_iota(I32, wide.shape, 0) + b * tb
            col = lax.broadcasted_iota(I32, wide.shape, 1)
            goal = jnp.sum(jnp.where(row == col, wide, 0.0), axis=1, keepdims=True)
            factor = goal * npts / total
            for i in range(nb):
                fout[b, :, i * bs : (i + 1) * bs] = xout[b, i] * factor

            @pl.when(b < last * per)
            def _():
                delivered(b).start()

            @pl.when(b >= last * per)
            def _():
                at = pl.multiple_of(lax.rem(b, per) * tb, tb)
                out[pl.ds(at, tb), :] = fout[b]

    make_table(0)

    @pl.when(s == 0)
    def _():
        enter(I32(0))
        make_table(1)
        prep(0)

    @pl.when(s > 0)
    def _():
        make_table(1)
        prep(0)
        prep(1)
        enter(I32(0))

    middle(I32(0))

    @pl.when(s == 0)
    def _():
        prep(1)

    def step(b, carry):
        enter(b)
        leave(b - 1)
        middle(b)
        finish(b - 1)
        return carry

    lax.fori_loop(1, nbatch, step, 0)
    leave(I32(nbatch - 1))
    finish(I32(nbatch - 1))

    pltpu.make_async_copy(crecv, crecv, c_send).wait()

    def drain(b, carry):
        for j in range(months):
            pltpu.make_async_copy(sendbuf.at[b, j], sendbuf.at[b, j], h_send.at[b, j]).wait()

        @pl.when(s < last)
        def _():
            passed(b).wait_send()

        @pl.when(s == last)
        def _():
            pltpu.make_async_copy(precv.at[b], precv.at[b], p_send.at[b]).wait()

            @pl.when(b < last * per)
            def _():
                delivered(b).wait_send()

        return carry

    lax.fori_loop(0, nbatch, drain, 0)

    @pl.when(s < last)
    def _():
        pltpu.make_async_copy(out, out, o_recv).wait()


def solution(mesh):
    sections, n = mesh.shape["month"], mesh.shape["grid"]

    def local(tracers, targets, retain, blocks, cols):
        months, nb, kk, bs = blocks.shape[:4]
        count, rows = tracers.shape
        nbatch = count // TB
        cap = -(-nb * FAR // (n - 1))
        slots = (n - 1) * cap
        dma = pltpu.SemaphoreType.DMA
        vmem = pl.BlockSpec(memory_space=pltpu.VMEM)
        return pl.pallas_call(
            functools.partial(kernel, sections, n, cap, months, nb, kk, bs, nbatch),
            out_shape=jax.ShapeDtypeStruct((count // sections, rows), F32),
            in_specs=[pl.BlockSpec(memory_space=pltpu.HBM)] * 5,
            out_specs=vmem,
            scratch_shapes=[
                pltpu.VMEM(tracers.shape, F32),
                pltpu.VMEM((1, count), F32),
                pltpu.VMEM(retain.shape, F32),
                pltpu.SMEM(cols.shape, I32),
                pltpu.VMEM((months, nb, kk, bs, bs), F32),
                pltpu.VMEM((months, nb, kk * bs, bs), BF16),
                pltpu.VMEM((months, nb, kk * bs, bs), BF16),
                pltpu.VMEM((nbatch, nb, TB, bs), F32),
                pltpu.VMEM((nbatch, nb, TB, bs), F32),
                pltpu.VMEM((nbatch, nb, TB, bs), F32),
                pltpu.VMEM((nb, 2 * TB, bs), BF16),
                pltpu.VMEM((nb, TB, bs), F32),
                pltpu.VMEM((slots, 2 * TB, bs), BF16),
                pltpu.VMEM((nb, TB, bs), F32),
                pltpu.VMEM((nbatch, months, slots, TB, bs), F32),
                pltpu.VMEM((nbatch, months, slots, TB, bs), F32),
                pltpu.VMEM((nbatch, TB, bs), F32),
                pltpu.VMEM((nbatch, n - 1, TB, bs), F32),
                pltpu.VMEM((nbatch, TB, rows), F32),
                pltpu.VMEM((n - 1,) + cols.shape, I32),
                pltpu.SMEM((n - 1,) + cols.shape, I32),
                pltpu.SMEM((months * slots,), I32),
                pltpu.SMEM((months * nb * FAR,), I32),
                dma((4,)), dma((months, nb)),
                dma, dma, dma,
                dma((nbatch, months)), dma((nbatch, months)),
                dma((nbatch,)), dma((nbatch,)),
                dma((nbatch,)), dma((nbatch,)),
                dma((nbatch,)), dma,
            ],
            compiler_params=pltpu.CompilerParams(
                collective_id=0, has_side_effects=True, vmem_limit_bytes=63 * 1024 * 1024 + 768 * 1024
            ),
        )(tracers, targets.reshape(1, -1), retain, blocks, cols)

    return jax.shard_map(
        local,
        mesh=mesh,
        in_specs=(
            P(None, "grid"),
            P(),
            P("month", "grid"),
            P("month", "grid", None, None, None),
            P("month", "grid", None),
        ),
        out_specs=P("month", "grid"),
        check_vma=False,
    )
```

```python
import functools

import jax
import jax.numpy as jnp
from jax import lax
from jax.experimental import pallas as pl
from jax.experimental.pallas import tpu as pltpu
from jax.sharding import PartitionSpec as P

FAR = 2
TB = 16
F32, BF16, I32 = jnp.float32, jnp.bfloat16, jnp.int32


def kernel(
    sections, n, cap, months, nb, kk, bs, nbatch,
    tracers_h, targets_h, retain_h, blocks, cols_h,
    out,
    tracers, targets, retain, cols_s,
    wf, whi, wlo, xin, xmid, xout, hl, cur, far, acc, sendbuf, recv, psend, precv, fout,
    crecv, csmem, send_tab, pos_tab,
    a_sem, w_sem, c_send, c_recv, c_loc, h_send, h_recv, in_send, in_recv, p_send, p_recv, o_send, o_recv,
):
    tb = TB
    near = kk - FAR
    per = nbatch // sections
    last = sections - 1
    nfar = nb * FAR
    npts = float(n * nb * bs)
    s = lax.axis_index("month")
    g = lax.axis_index("grid")
    offsets = sorted(range(1, n), key=lambda o: abs(o - n // 2))

    def peer(o):
        return lax.rem(g + o, n)

    def chunk(j, i):
        return pltpu.make_async_copy(blocks.at[j, i], wf.at[j, i], w_sem.at[j, i])

    get_cols = pltpu.make_async_copy(cols_h, cols_s, a_sem.at[0])
    get_tracers = pltpu.make_async_copy(tracers_h, tracers, a_sem.at[1])
    get_retain = pltpu.make_async_copy(retain_h, retain, a_sem.at[2])
    get_targets = pltpu.make_async_copy(targets_h, targets, a_sem.at[3])
    get_cols.start()
    get_tracers.start()
    get_retain.start()
    get_targets.start()
    for j in range(months):
        for i in range(nb):
            chunk(j, i).start()

    barrier = pltpu.get_barrier_semaphore()
    for o in range(1, n):
        pl.semaphore_signal(barrier, inc=1, device_id={"grid": peer(o)}, device_id_type=pl.DeviceIdType.MESH)
    for o in range(1, sections):
        pl.semaphore_signal(
            barrier, inc=1, device_id={"month": lax.rem(s + o, sections)}, device_id_type=pl.DeviceIdType.MESH
        )
    pl.semaphore_wait(barrier, n - 1 + sections - 1)

    for o in offsets:
        pltpu.make_async_remote_copy(
            cols_h, crecv.at[o - 1], c_send, c_recv,
            device_id={"grid": peer(o)}, device_id_type=pl.DeviceIdType.MESH,
        ).start()

    get_cols.wait()
    get_tracers.wait()
    get_retain.wait()
    get_targets.wait()

    @pl.when(s == 0)
    def _():
        for b in range(nbatch):
            for i in range(nb):
                xin[b, i] = tracers[b * tb : (b + 1) * tb, i * bs : (i + 1) * bs]

    def far_at(j, e):
        return j, e // FAR, near + e % FAR

    for j in range(months):
        owners = [cols_s[far_at(j, e)] // nb for e in range(nfar)]
        for e in range(nfar):
            rank = I32(0)
            for f in range(e):
                rank = rank + jnp.where(owners[f] == owners[e], 1, 0)
            off = g - owners[e]
            off = jnp.where(off < 0, off + n, off)
            pos_tab[j * nfar + e] = jnp.clip((off - 1) * cap + rank, 0, (n - 1) * cap - 1)

    pltpu.make_async_copy(crecv, crecv, c_recv).wait()
    local = pltpu.make_async_copy(crecv, csmem, c_loc)
    local.start()
    local.wait()

    def make_table(j):
        def one(q, carry):
            o = q + 1
            count = I32(0)
            idx = [I32(0)] * cap
            for e in range(nfar):
                c = csmem[(n - 1 - o,) + far_at(j, e)] - g * nb
                hit = (c >= 0) & (c < nb)
                for r in range(cap):
                    idx[r] = jnp.where(hit & (count == r), c, idx[r])
                count = count + jnp.where(hit, 1, 0)
            for r in range(cap):
                send_tab[(j * (n - 1) + q) * cap + r] = idx[r]
            return carry

        lax.fori_loop(0, n - 1, one, 0)

    def prep(j):
        def one(i, carry):
            chunk(j, i).wait()
            for k in range(kk):
                b = wf[j, i, k].T
                hi = b.astype(BF16)
                whi[j, i, k * bs : (k + 1) * bs, :] = hi
                wlo[j, i, k * bs : (k + 1) * bs, :] = (b - hi.astype(F32)).astype(BF16)
            return carry

        lax.fori_loop(0, nb, one, 0)

    def split(v):
        hi = v.astype(BF16).astype(F32)
        return jnp.concatenate([hi, v - hi], axis=0).astype(BF16)

    def product(rows, j, i, lo, hi):
        d = jnp.dot(rows, whi[j, i, lo * bs : hi * bs, :], preferred_element_type=F32)
        d = d + jnp.dot(rows, wlo[j, i, lo * bs : hi * bs, :], preferred_element_type=F32)
        return d[:tb] + d[tb:]

    def send_halo(b, j, src):
        for i in range(nb):
            cur[i] = src[b, i]
        for o in offsets:
            for r in range(cap):
                q = (o - 1) * cap + r
                idx = send_tab[j * (n - 1) * cap + q]
                sendbuf[b, j, q] = cur[idx]
            pltpu.make_async_remote_copy(
                sendbuf.at[b, j, pl.ds((o - 1) * cap, cap)],
                recv.at[b, j, pl.ds((o - 1) * cap, cap)],
                h_send.at[b, j], h_recv.at[b, j],
                device_id={"grid": peer(o)}, device_id_type=pl.DeviceIdType.MESH,
            ).start()

    def apply(b, j, src, dst):
        for i in range(nb):
            hl[i] = split(src[b, i])
        for i in range(nb):
            picked = [hl[i]]
            for k in range(1, near):
                picked.append(hl[jnp.clip(cols_s[j, i, k] - g * nb, 0, nb - 1)])
            rows = jnp.concatenate(picked, axis=1)
            keep = retain[j : j + 1, i * bs : (i + 1) * bs]
            acc[i] = keep * src[b, i] + product(rows, j, i, 0, near)
        pltpu.make_async_copy(recv.at[b, j], recv.at[b, j], h_recv.at[b, j]).wait()
        for q in range((n - 1) * cap):
            far[q] = split(recv[b, j, q])
        for i in range(nb):
            rows = jnp.concatenate([far[pos_tab[j * nfar + i * FAR + f]] for f in range(FAR)], axis=1)
            dst[b, i] = acc[i] + product(rows, j, i, near, kk)

    def enter(b):
        @pl.when(s > 0)
        def _():
            pltpu.make_async_copy(xin.at[b], xin.at[b], in_recv.at[b]).wait()

        send_halo(b, 0, xin)

    def middle(b):
        apply(b, 0, xin, xmid)
        send_halo(b, 1, xmid)

    def passed(b):
        return pltpu.make_async_remote_copy(
            xout.at[b], xin.at[b], in_send.at[b], in_recv.at[b],
            device_id={"month": lax.rem(s + 1, sections)}, device_id_type=pl.DeviceIdType.MESH,
        )

    def leave(b):
        apply(b, 1, xmid, xout)

        @pl.when(s < last)
        def _():
            passed(b).start()

        @pl.when(s == last)
        def _():
            total = xout[b, 0]
            for i in range(1, nb):
                total = total + xout[b, i]
            psend[b] = jnp.broadcast_to(jnp.sum(total, axis=1, keepdims=True), (tb, bs))
            for o in offsets:
                pltpu.make_async_remote_copy(
                    psend.at[b], precv.at[b, o - 1], p_send.at[b], p_recv.at[b],
                    device_id={"grid": peer(o)}, device_id_type=pl.DeviceIdType.MESH,
                ).start()

    def delivered(b):
        row = pl.multiple_of(lax.rem(b, per) * tb, tb)
        return pltpu.make_async_remote_copy(
            fout.at[b], out.at[pl.ds(row, tb)], o_send.at[b], o_recv,
            device_id={"month": lax.div(b, per)}, device_id_type=pl.DeviceIdType.MESH,
        )

    def finish(b):
        @pl.when(s == last)
        def _():
            pltpu.make_async_copy(precv.at[b], precv.at[b], p_recv.at[b]).wait()
            total = psend[b]
            for o in range(1, n):
                total = total + precv[b, o - 1]
            wide = jnp.broadcast_to(targets[...], (tb, targets.shape[1]))
            row = lax.broadcasted_iota(I32, wide.shape, 0) + b * tb
            col = lax.broadcasted_iota(I32, wide.shape, 1)
            goal = jnp.sum(jnp.where(row == col, wide, 0.0), axis=1, keepdims=True)
            factor = goal * npts / total
            for i in range(nb):
                fout[b, :, i * bs : (i + 1) * bs] = xout[b, i] * factor

            @pl.when(b < last * per)
            def _():
                delivered(b).start()

            @pl.when(b >= last * per)
            def _():
                at = pl.multiple_of(lax.rem(b, per) * tb, tb)
                out[pl.ds(at, tb), :] = fout[b]

    make_table(0)

    @pl.when(s == 0)
    def _():
        enter(I32(0))
        make_table(1)
        prep(0)

    @pl.when(s > 0)
    def _():
        make_table(1)
        prep(0)
        prep(1)
        enter(I32(0))

    middle(I32(0))

    @pl.when(s == 0)
    def _():
        prep(1)

    def step(b, carry):
        enter(b)
        leave(b - 1)
        middle(b)
        finish(b - 1)
        return carry

    lax.fori_loop(1, nbatch, step, 0)
    leave(I32(nbatch - 1))
    finish(I32(nbatch - 1))

    pltpu.make_async_copy(crecv, crecv, c_send).wait()

    def drain(b, carry):
        for j in range(months):
            pltpu.make_async_copy(sendbuf.at[b, j], sendbuf.at[b, j], h_send.at[b, j]).wait()

        @pl.when(s < last)
        def _():
            passed(b).wait_send()

        @pl.when(s == last)
        def _():
            pltpu.make_async_copy(precv.at[b], precv.at[b], p_send.at[b]).wait()

            @pl.when(b < last * per)
            def _():
                delivered(b).wait_send()

        return carry

    lax.fori_loop(0, nbatch, drain, 0)

    @pl.when(s < last)
    def _():
        pltpu.make_async_copy(out, out, o_recv).wait()


def solution(mesh):
    sections, n = mesh.shape["month"], mesh.shape["grid"]

    def local(tracers, targets, retain, blocks, cols):
        months, nb, kk, bs = blocks.shape[:4]
        count, rows = tracers.shape
        nbatch = count // TB
        cap = -(-nb * FAR // (n - 1))
        slots = (n - 1) * cap
        dma = pltpu.SemaphoreType.DMA
        vmem = pl.BlockSpec(memory_space=pltpu.VMEM)
        return pl.pallas_call(
            functools.partial(kernel, sections, n, cap, months, nb, kk, bs, nbatch),
            out_shape=jax.ShapeDtypeStruct((count // sections, rows), F32),
            in_specs=[pl.BlockSpec(memory_space=pltpu.HBM)] * 5,
            out_specs=vmem,
            scratch_shapes=[
                pltpu.VMEM(tracers.shape, F32),
                pltpu.VMEM((1, count), F32),
                pltpu.VMEM(retain.shape, F32),
                pltpu.SMEM(cols.shape, I32),
                pltpu.VMEM((months, nb, kk, bs, bs), F32),
                pltpu.VMEM((months, nb, kk * bs, bs), BF16),
                pltpu.VMEM((months, nb, kk * bs, bs), BF16),
                pltpu.VMEM((nbatch, nb, TB, bs), F32),
                pltpu.VMEM((nbatch, nb, TB, bs), F32),
                pltpu.VMEM((nbatch, nb, TB, bs), F32),
                pltpu.VMEM((nb, 2 * TB, bs), BF16),
                pltpu.VMEM((nb, TB, bs), F32),
                pltpu.VMEM((slots, 2 * TB, bs), BF16),
                pltpu.VMEM((nb, TB, bs), F32),
                pltpu.VMEM((nbatch, months, slots, TB, bs), F32),
                pltpu.VMEM((nbatch, months, slots, TB, bs), F32),
                pltpu.VMEM((nbatch, TB, bs), F32),
                pltpu.VMEM((nbatch, n - 1, TB, bs), F32),
                pltpu.VMEM((nbatch, TB, rows), F32),
                pltpu.VMEM((n - 1,) + cols.shape, I32),
                pltpu.SMEM((n - 1,) + cols.shape, I32),
                pltpu.SMEM((months * slots,), I32),
                pltpu.SMEM((months * nb * FAR,), I32),
                dma((4,)), dma((months, nb)),
                dma, dma, dma,
                dma((nbatch, months)), dma((nbatch, months)),
                dma((nbatch,)), dma((nbatch,)),
                dma((nbatch,)), dma((nbatch,)),
                dma((nbatch,)), dma,
            ],
            compiler_params=pltpu.CompilerParams(
                collective_id=0, has_side_effects=True, vmem_limit_bytes=63 * 1024 * 1024 + 768 * 1024
            ),
        )(tracers, targets.reshape(1, -1), retain, blocks, cols)

    return jax.shard_map(
        local,
        mesh=mesh,
        in_specs=(
            P(None, "grid"),
            P(),
            P("month", "grid"),
            P("month", "grid", None, None, None),
            P("month", "grid", None),
        ),
        out_specs=P("month", "grid"),
        check_vma=False,
    )
```

```python
import functools

import jax
import jax.numpy as jnp
from jax import lax
from jax.experimental import pallas as pl
from jax.experimental.pallas import tpu as pltpu
from jax.sharding import PartitionSpec as P

FAR = 2
TB = 8
F32, BF16, I32 = jnp.float32, jnp.bfloat16, jnp.int32


def kernel(
    sections, n, cap, months, nb, kk, bs, nbatch,
    tracers_h, targets_h, retain_h, blocks, cols_h,
    out,
    tracers, targets, retain, cols_s,
    wf, whi, wlo, xin, xmid, xout, hl, cur, far, acc, sendbuf, recv, psend, precv, fout,
    crecv, csmem, send_tab, pos_tab,
    a_sem, w_sem, c_send, c_recv, c_loc, h_send, h_recv, in_send, in_recv, p_send, p_recv, o_send, o_recv,
):
    tb = TB
    near = kk - FAR
    per = nbatch // sections
    last = sections - 1
    nfar = nb * FAR
    npts = float(n * nb * bs)
    s = lax.axis_index("month")
    g = lax.axis_index("grid")
    offsets = sorted(range(1, n), key=lambda o: abs(o - n // 2))

    def peer(o):
        return lax.rem(g + o, n)

    def chunk(j, i):
        return pltpu.make_async_copy(blocks.at[j, i], wf.at[j, i], w_sem.at[j, i])

    get_cols = pltpu.make_async_copy(cols_h, cols_s, a_sem.at[0])
    get_tracers = pltpu.make_async_copy(tracers_h, tracers, a_sem.at[1])
    get_retain = pltpu.make_async_copy(retain_h, retain, a_sem.at[2])
    get_targets = pltpu.make_async_copy(targets_h, targets, a_sem.at[3])
    get_cols.start()
    get_tracers.start()
    get_retain.start()
    get_targets.start()
    for j in range(months):
        for i in range(nb):
            chunk(j, i).start()

    barrier = pltpu.get_barrier_semaphore()
    for d in range(sections):
        for o in range(n):
            if d + o > 0:
                pl.semaphore_signal(
                    barrier, inc=1, device_id={"month": lax.rem(s + d, sections), "grid": peer(o)},
                    device_id_type=pl.DeviceIdType.MESH,
                )
    pl.semaphore_wait(barrier, n * sections - 1)

    for o in offsets:
        for group in range(2):
            pltpu.make_async_remote_copy(
                cols_h, crecv.at[group, o - 1], c_send, c_recv,
                device_id={"month": lax.rem(s + group * (sections - 1), sections), "grid": peer(o)},
                device_id_type=pl.DeviceIdType.MESH,
            ).start()

    get_cols.wait()
    get_tracers.wait()
    get_retain.wait()
    get_targets.wait()

    @pl.when(s == 0)
    def _():
        for b in range(nbatch):
            for i in range(nb):
                xin[b, i] = tracers[b * tb : (b + 1) * tb, i * bs : (i + 1) * bs]

    def far_at(j, e):
        return j, e // FAR, near + e % FAR

    for j in range(months):
        owners = [cols_s[far_at(j, e)] // nb for e in range(nfar)]
        for e in range(nfar):
            rank = I32(0)
            for f in range(e):
                rank = rank + jnp.where(owners[f] == owners[e], 1, 0)
            off = g - owners[e]
            off = jnp.where(off < 0, off + n, off)
            pos_tab[j * nfar + e] = jnp.clip((off - 1) * cap + rank, 0, (n - 1) * cap - 1)

    pltpu.make_async_copy(crecv, crecv, c_recv).wait()
    local = pltpu.make_async_copy(crecv, csmem, c_loc)
    local.start()
    local.wait()

    def make_table(j):
        def one(q, carry):
            o = q + 1
            count = I32(0)
            idx = [I32(0)] * cap
            for e in range(nfar):
                c = csmem[(1 - j, n - 1 - o) + far_at(j, e)] - g * nb
                hit = (c >= 0) & (c < nb)
                for r in range(cap):
                    idx[r] = jnp.where(hit & (count == r), c, idx[r])
                count = count + jnp.where(hit, 1, 0)
            for r in range(cap):
                send_tab[(j * (n - 1) + q) * cap + r] = idx[r]
            return carry

        lax.fori_loop(0, n - 1, one, 0)

    def prep(j):
        def one(i, carry):
            chunk(j, i).wait()
            for k in range(kk):
                b = wf[j, i, k].T
                hi = b.astype(BF16)
                whi[j, i, k * bs : (k + 1) * bs, :] = hi
                wlo[j, i, k * bs : (k + 1) * bs, :] = (b - hi.astype(F32)).astype(BF16)
            return carry

        lax.fori_loop(0, nb, one, 0)

    def split(v):
        hi = v.astype(BF16).astype(F32)
        return jnp.concatenate([hi, v - hi], axis=0).astype(BF16)

    def product(rows, j, i, lo, hi):
        d = jnp.dot(rows, whi[j, i, lo * bs : hi * bs, :], preferred_element_type=F32)
        d = d + jnp.dot(rows, wlo[j, i, lo * bs : hi * bs, :], preferred_element_type=F32)
        return d[:tb] + d[tb:]

    def send_halo(b, j, part):
        for i in range(nb):
            cur[i] = part(i)
        goal = lax.rem(s + 1 - j, sections)
        for o in offsets:
            for r in range(cap):
                q = (o - 1) * cap + r
                idx = send_tab[j * (n - 1) * cap + q]
                sendbuf[b, j, q] = cur[idx]
            pltpu.make_async_remote_copy(
                sendbuf.at[b, j, pl.ds((o - 1) * cap, cap)],
                recv.at[b, j, pl.ds((o - 1) * cap, cap)],
                h_send.at[b, j], h_recv.at[b, j],
                device_id={"month": goal, "grid": peer(o)}, device_id_type=pl.DeviceIdType.MESH,
            ).start()

    def apply(b, j, src, dst):
        for i in range(nb):
            hl[i] = split(src[b, i])
        for i in range(nb):
            picked = [hl[i]]
            for k in range(1, near):
                picked.append(hl[jnp.clip(cols_s[j, i, k] - g * nb, 0, nb - 1)])
            rows = jnp.concatenate(picked, axis=1)
            keep = retain[j : j + 1, i * bs : (i + 1) * bs]
            acc[i] = keep * src[b, i] + product(rows, j, i, 0, near)
        pltpu.make_async_copy(recv.at[b, j], recv.at[b, j], h_recv.at[b, j]).wait()
        for q in range((n - 1) * cap):
            far[q] = split(recv[b, j, q])
        for i in range(nb):
            rows = jnp.concatenate([far[pos_tab[j * nfar + i * FAR + f]] for f in range(FAR)], axis=1)
            dst[b, i] = acc[i] + product(rows, j, i, near, kk)

    def middle(b):
        @pl.when(s > 0)
        def _():
            pltpu.make_async_copy(xin.at[b], xin.at[b], in_recv.at[b]).wait()

        apply(b, 0, xin, xmid)
        send_halo(b, 1, lambda i: xmid[b, i])

    def passed(b):
        return pltpu.make_async_remote_copy(
            xout.at[b], xin.at[b], in_send.at[b], in_recv.at[b],
            device_id={"month": lax.rem(s + 1, sections)}, device_id_type=pl.DeviceIdType.MESH,
        )

    def leave(b):
        apply(b, 1, xmid, xout)

        @pl.when(s < last)
        def _():
            passed(b).start()
            send_halo(b, 0, lambda i: xout[b, i])

        @pl.when(s == last)
        def _():
            total = xout[b, 0]
            for i in range(1, nb):
                total = total + xout[b, i]
            psend[b] = jnp.broadcast_to(jnp.sum(total, axis=1, keepdims=True), (tb, bs))
            for o in offsets:
                pltpu.make_async_remote_copy(
                    psend.at[b], precv.at[b, o - 1], p_send.at[b], p_recv.at[b],
                    device_id={"grid": peer(o)}, device_id_type=pl.DeviceIdType.MESH,
                ).start()

    def delivered(b):
        row = pl.multiple_of(lax.rem(b, per) * tb, tb)
        return pltpu.make_async_remote_copy(
            fout.at[b], out.at[pl.ds(row, tb)], o_send.at[b], o_recv,
            device_id={"month": lax.div(b, per)}, device_id_type=pl.DeviceIdType.MESH,
        )

    def finish(b):
        @pl.when(s == last)
        def _():
            pltpu.make_async_copy(precv.at[b], precv.at[b], p_recv.at[b]).wait()
            total = psend[b]
            for o in range(1, n):
                total = total + precv[b, o - 1]
            wide = jnp.broadcast_to(targets[...], (tb, targets.shape[1]))
            row = lax.broadcasted_iota(I32, wide.shape, 0) + b * tb
            col = lax.broadcasted_iota(I32, wide.shape, 1)
            goal = jnp.sum(jnp.where(row == col, wide, 0.0), axis=1, keepdims=True)
            factor = goal * npts / total
            for i in range(nb):
                fout[b, :, i * bs : (i + 1) * bs] = xout[b, i] * factor

            @pl.when(b < last * per)
            def _():
                delivered(b).start()

            @pl.when(b >= last * per)
            def _():
                at = pl.multiple_of(lax.rem(b, per) * tb, tb)
                out[pl.ds(at, tb), :] = fout[b]

    make_table(0)

    @pl.when(s == last)
    def _():
        def one(b, carry):
            at = pl.multiple_of(b * tb, tb)
            send_halo(b, 0, lambda i: tracers[pl.ds(at, tb), i * bs : (i + 1) * bs])
            return carry

        lax.fori_loop(0, nbatch, one, 0)

    make_table(1)
    prep(0)

    @pl.when(s > 0)
    def _():
        prep(1)

    middle(I32(0))

    @pl.when(s == 0)
    def _():
        prep(1)

    def step(b, carry):
        middle(b)

        @pl.when(b >= 2)
        def _():
            finish(b - 2)

        leave(b - 1)
        return carry

    lax.fori_loop(1, nbatch, step, 0)
    leave(I32(nbatch - 1))
    finish(I32(nbatch - 2))
    finish(I32(nbatch - 1))

    pltpu.make_async_copy(crecv, crecv, c_send).wait()

    def drain(b, carry):
        for j in range(months):
            pltpu.make_async_copy(sendbuf.at[b, j], sendbuf.at[b, j], h_send.at[b, j]).wait()

        @pl.when(s < last)
        def _():
            passed(b).wait_send()

        @pl.when(s == last)
        def _():
            pltpu.make_async_copy(precv.at[b], precv.at[b], p_send.at[b]).wait()

            @pl.when(b < last * per)
            def _():
                delivered(b).wait_send()

        return carry

    lax.fori_loop(0, nbatch, drain, 0)

    @pl.when(s < last)
    def _():
        pltpu.make_async_copy(out, out, o_recv).wait()


def solution(mesh):
    sections, n = mesh.shape["month"], mesh.shape["grid"]

    def local(tracers, targets, retain, blocks, cols):
        months, nb, kk, bs = blocks.shape[:4]
        count, rows = tracers.shape
        nbatch = count // TB
        cap = -(-nb * FAR // (n - 1))
        slots = (n - 1) * cap
        dma = pltpu.SemaphoreType.DMA
        vmem = pl.BlockSpec(memory_space=pltpu.VMEM)
        return pl.pallas_call(
            functools.partial(kernel, sections, n, cap, months, nb, kk, bs, nbatch),
            out_shape=jax.ShapeDtypeStruct((count // sections, rows), F32),
            in_specs=[pl.BlockSpec(memory_space=pltpu.HBM)] * 5,
            out_specs=vmem,
            scratch_shapes=[
                pltpu.VMEM(tracers.shape, F32),
                pltpu.VMEM((1, count), F32),
                pltpu.VMEM(retain.shape, F32),
                pltpu.SMEM(cols.shape, I32),
                pltpu.VMEM((months, nb, kk, bs, bs), F32),
                pltpu.VMEM((months, nb, kk * bs, bs), BF16),
                pltpu.VMEM((months, nb, kk * bs, bs), BF16),
                pltpu.VMEM((nbatch, nb, TB, bs), F32),
                pltpu.VMEM((nbatch, nb, TB, bs), F32),
                pltpu.VMEM((nbatch, nb, TB, bs), F32),
                pltpu.VMEM((nb, 2 * TB, bs), BF16),
                pltpu.VMEM((nb, TB, bs), F32),
                pltpu.VMEM((slots, 2 * TB, bs), BF16),
                pltpu.VMEM((nb, TB, bs), F32),
                pltpu.VMEM((nbatch, months, slots, TB, bs), F32),
                pltpu.VMEM((nbatch, months, slots, TB, bs), F32),
                pltpu.VMEM((nbatch, TB, bs), F32),
                pltpu.VMEM((nbatch, n - 1, TB, bs), F32),
                pltpu.VMEM((nbatch, TB, rows), F32),
                pltpu.VMEM((2, n - 1) + cols.shape, I32),
                pltpu.SMEM((2, n - 1) + cols.shape, I32),
                pltpu.SMEM((months * slots,), I32),
                pltpu.SMEM((months * nb * FAR,), I32),
                dma((4,)), dma((months, nb)),
                dma, dma, dma,
                dma((nbatch, months)), dma((nbatch, months)),
                dma((nbatch,)), dma((nbatch,)),
                dma((nbatch,)), dma((nbatch,)),
                dma((nbatch,)), dma,
            ],
            compiler_params=pltpu.CompilerParams(
                collective_id=0, has_side_effects=True, vmem_limit_bytes=63 * 1024 * 1024 + 768 * 1024
            ),
        )(tracers, targets.reshape(1, -1), retain, blocks, cols)

    return jax.shard_map(
        local,
        mesh=mesh,
        in_specs=(
            P(None, "grid"),
            P(),
            P("month", "grid"),
            P("month", "grid", None, None, None),
            P("month", "grid", None),
        ),
        out_specs=P("month", "grid"),
        check_vma=False,
    )
```

```python
import functools

import jax
import jax.numpy as jnp
from jax import lax
from jax.experimental import pallas as pl
from jax.experimental.pallas import tpu as pltpu
from jax.sharding import PartitionSpec as P

FAR = 2
TB = 8
F32, BF16, I32 = jnp.float32, jnp.bfloat16, jnp.int32


def kernel(
    sections, n, cap, months, nb, kk, bs, nbatch,
    tracers_h, targets_h, retain_h, blocks, cols_h,
    out,
    tracers, targets, retain, cols_s,
    wf, whi, wlo, xin, xmid, xout, hl, cur, far, acc, sendbuf, recv, psend, precv, fout,
    crecv, csmem, send_tab, pos_tab,
    a_sem, w_sem, c_send, c_recv, c_loc, h_send, h_recv, in_send, in_recv, p_send, p_recv, o_send, o_recv,
):
    tb = TB
    near = kk - FAR
    per = nbatch // sections
    last = sections - 1
    nfar = nb * FAR
    npts = float(n * nb * bs)
    s = lax.axis_index("month")
    g = lax.axis_index("grid")
    offsets = sorted(range(1, n), key=lambda o: abs(o - n // 2))

    def peer(o):
        return lax.rem(g + o, n)

    def chunk(j, i):
        return pltpu.make_async_copy(blocks.at[j, i], wf.at[j, i], w_sem.at[j, i])

    get_cols = pltpu.make_async_copy(cols_h, cols_s, a_sem.at[0])
    get_tracers = pltpu.make_async_copy(tracers_h, tracers, a_sem.at[1])
    get_retain = pltpu.make_async_copy(retain_h, retain, a_sem.at[2])
    get_targets = pltpu.make_async_copy(targets_h, targets, a_sem.at[3])
    get_cols.start()
    get_tracers.start()
    get_retain.start()
    get_targets.start()
    for j in range(months):
        for i in range(nb):
            chunk(j, i).start()

    barrier = pltpu.get_barrier_semaphore()
    for d in range(sections):
        for o in range(n):
            if d + o > 0:
                pl.semaphore_signal(
                    barrier, inc=1, device_id={"month": lax.rem(s + d, sections), "grid": peer(o)},
                    device_id_type=pl.DeviceIdType.MESH,
                )
    pl.semaphore_wait(barrier, n * sections - 1)

    for o in offsets:
        for group in range(2):
            pltpu.make_async_remote_copy(
                cols_h, crecv.at[group, o - 1], c_send, c_recv,
                device_id={"month": lax.rem(s + group * (sections - 1), sections), "grid": peer(o)},
                device_id_type=pl.DeviceIdType.MESH,
            ).start()

    get_cols.wait()
    get_tracers.wait()
    get_retain.wait()
    get_targets.wait()

    @pl.when(s == 0)
    def _():
        for b in range(nbatch):
            for i in range(nb):
                xin[b, i] = tracers[b * tb : (b + 1) * tb, i * bs : (i + 1) * bs]

    def far_at(j, e):
        return j, e // FAR, near + e % FAR

    for j in range(months):
        owners = [cols_s[far_at(j, e)] // nb for e in range(nfar)]
        for e in range(nfar):
            rank = I32(0)
            for f in range(e):
                rank = rank + jnp.where(owners[f] == owners[e], 1, 0)
            off = g - owners[e]
            off = jnp.where(off < 0, off + n, off)
            pos_tab[j * nfar + e] = jnp.clip((off - 1) * cap + rank, 0, (n - 1) * cap - 1)

    pltpu.make_async_copy(crecv, crecv, c_recv).wait()
    local = pltpu.make_async_copy(crecv, csmem, c_loc)
    local.start()
    local.wait()

    def make_table(t, group, j):
        def one(q, carry):
            o = q + 1
            count = I32(0)
            idx = [I32(0)] * cap
            for e in range(nfar):
                c = csmem[(group, n - 1 - o) + far_at(j, e)] - g * nb
                hit = (c >= 0) & (c < nb)
                for r in range(cap):
                    idx[r] = jnp.where(hit & (count == r), c, idx[r])
                count = count + jnp.where(hit, 1, 0)
            for r in range(cap):
                send_tab[(t * (n - 1) + q) * cap + r] = idx[r]
            return carry

        lax.fori_loop(0, n - 1, one, 0)

    def prep(j):
        def one(i, carry):
            chunk(j, i).wait()
            for k in range(kk):
                b = wf[j, i, k].T
                hi = b.astype(BF16)
                whi[j, i, k * bs : (k + 1) * bs, :] = hi
                wlo[j, i, k * bs : (k + 1) * bs, :] = (b - hi.astype(F32)).astype(BF16)
            return carry

        lax.fori_loop(0, nb, one, 0)

    def split(v):
        hi = v.astype(BF16).astype(F32)
        return jnp.concatenate([hi, v - hi], axis=0).astype(BF16)

    def product(rows, j, i, lo, hi):
        d = jnp.dot(rows, whi[j, i, lo * bs : hi * bs, :], preferred_element_type=F32)
        d = d + jnp.dot(rows, wlo[j, i, lo * bs : hi * bs, :], preferred_element_type=F32)
        return d[:tb] + d[tb:]

    def send_halo(b, t, part):
        for i in range(nb):
            cur[i] = part(i)
        j = t % 2
        goal = lax.rem(s + (t == 0), sections)
        for o in offsets:
            for r in range(cap):
                q = (o - 1) * cap + r
                idx = send_tab[t * (n - 1) * cap + q]
                sendbuf[b, t, q] = cur[idx]
            pltpu.make_async_remote_copy(
                sendbuf.at[b, t, pl.ds((o - 1) * cap, cap)],
                recv.at[b, j, pl.ds((o - 1) * cap, cap)],
                h_send.at[b, t], h_recv.at[b, j],
                device_id={"month": goal, "grid": peer(o)}, device_id_type=pl.DeviceIdType.MESH,
            ).start()

    def apply(b, j, src, dst):
        for i in range(nb):
            hl[i] = split(src[b, i])
        for i in range(nb):
            picked = [hl[i]]
            for k in range(1, near):
                picked.append(hl[jnp.clip(cols_s[j, i, k] - g * nb, 0, nb - 1)])
            rows = jnp.concatenate(picked, axis=1)
            keep = retain[j : j + 1, i * bs : (i + 1) * bs]
            acc[i] = keep * src[b, i] + product(rows, j, i, 0, near)
        pltpu.make_async_copy(recv.at[b, j], recv.at[b, j], h_recv.at[b, j]).wait()
        for q in range((n - 1) * cap):
            far[q] = split(recv[b, j, q])
        for i in range(nb):
            rows = jnp.concatenate([far[pos_tab[j * nfar + i * FAR + f]] for f in range(FAR)], axis=1)
            dst[b, i] = acc[i] + product(rows, j, i, near, kk)

    def middle(b):
        @pl.when(s > 0)
        def _():
            pltpu.make_async_copy(xin.at[b], xin.at[b], in_recv.at[b]).wait()

        apply(b, 0, xin, xmid)
        send_halo(b, 1, lambda i: xmid[b, i])

    def passed(b):
        return pltpu.make_async_remote_copy(
            xout.at[b], xin.at[b], in_send.at[b], in_recv.at[b],
            device_id={"month": lax.rem(s + 1, sections)}, device_id_type=pl.DeviceIdType.MESH,
        )

    def leave(b):
        apply(b, 1, xmid, xout)

        @pl.when(s < last)
        def _():
            passed(b).start()
            send_halo(b, 0, lambda i: xout[b, i])

        @pl.when(s == last)
        def _():
            total = xout[b, 0]
            for i in range(1, nb):
                total = total + xout[b, i]
            psend[b] = jnp.broadcast_to(jnp.sum(total, axis=1, keepdims=True), (tb, bs))
            for o in offsets:
                pltpu.make_async_remote_copy(
                    psend.at[b], precv.at[b, o - 1], p_send.at[b], p_recv.at[b],
                    device_id={"grid": peer(o)}, device_id_type=pl.DeviceIdType.MESH,
                ).start()

    def delivered(b):
        row = pl.multiple_of(lax.rem(b, per) * tb, tb)
        return pltpu.make_async_remote_copy(
            fout.at[b], out.at[pl.ds(row, tb)], o_send.at[b], o_recv,
            device_id={"month": lax.div(b, per)}, device_id_type=pl.DeviceIdType.MESH,
        )

    def finish(b):
        @pl.when(s == last)
        def _():
            pltpu.make_async_copy(precv.at[b], precv.at[b], p_recv.at[b]).wait()
            total = psend[b]
            for o in range(1, n):
                total = total + precv[b, o - 1]
            wide = jnp.broadcast_to(targets[...], (tb, targets.shape[1]))
            row = lax.broadcasted_iota(I32, wide.shape, 0) + b * tb
            col = lax.broadcasted_iota(I32, wide.shape, 1)
            goal = jnp.sum(jnp.where(row == col, wide, 0.0), axis=1, keepdims=True)
            factor = goal * npts / total
            for i in range(nb):
                fout[b, :, i * bs : (i + 1) * bs] = xout[b, i] * factor

            @pl.when(b < last * per)
            def _():
                delivered(b).start()

            @pl.when(b >= last * per)
            def _():
                at = pl.multiple_of(lax.rem(b, per) * tb, tb)
                out[pl.ds(at, tb), :] = fout[b]

    def first(b):
        at = pl.multiple_of(b * tb, tb)
        send_halo(b, 2, lambda i: tracers[pl.ds(at, tb), i * bs : (i + 1) * bs])

    @pl.when(s == 0)
    def _():
        make_table(2, 0, 0)
        first(I32(0))

    make_table(0, 1, 0)
    make_table(1, 0, 1)
    prep(0)

    @pl.when(s > 0)
    def _():
        prep(1)

    middle(I32(0))

    @pl.when(s == 0)
    def _():
        first(I32(1))
        prep(1)

    def step(b, carry):
        middle(b)

        @pl.when((s == 0) & (b < nbatch - 1))
        def _():
            first(b + 1)

        @pl.when(b >= 2)
        def _():
            finish(b - 2)

        leave(b - 1)
        return carry

    lax.fori_loop(1, nbatch, step, 0)
    leave(I32(nbatch - 1))
    finish(I32(nbatch - 2))
    finish(I32(nbatch - 1))

    pltpu.make_async_copy(crecv, crecv, c_send).wait()

    def drain(b, carry):
        def sent(t):
            pltpu.make_async_copy(sendbuf.at[b, t], sendbuf.at[b, t], h_send.at[b, t]).wait()

        sent(1)

        @pl.when(s < last)
        def _():
            sent(0)

        @pl.when(s == 0)
        def _():
            sent(2)

        @pl.when(s < last)
        def _():
            passed(b).wait_send()

        @pl.when(s == last)
        def _():
            pltpu.make_async_copy(precv.at[b], precv.at[b], p_send.at[b]).wait()

            @pl.when(b < last * per)
            def _():
                delivered(b).wait_send()

        return carry

    lax.fori_loop(0, nbatch, drain, 0)

    @pl.when(s < last)
    def _():
        pltpu.make_async_copy(out, out, o_recv).wait()


def solution(mesh):
    sections, n = mesh.shape["month"], mesh.shape["grid"]

    def local(tracers, targets, retain, blocks, cols):
        months, nb, kk, bs = blocks.shape[:4]
        count, rows = tracers.shape
        nbatch = count // TB
        cap = -(-nb * FAR // (n - 1))
        slots = (n - 1) * cap
        dma = pltpu.SemaphoreType.DMA
        vmem = pl.BlockSpec(memory_space=pltpu.VMEM)
        return pl.pallas_call(
            functools.partial(kernel, sections, n, cap, months, nb, kk, bs, nbatch),
            out_shape=jax.ShapeDtypeStruct((count // sections, rows), F32),
            in_specs=[pl.BlockSpec(memory_space=pltpu.HBM)] * 5,
            out_specs=vmem,
            scratch_shapes=[
                pltpu.VMEM(tracers.shape, F32),
                pltpu.VMEM((1, count), F32),
                pltpu.VMEM(retain.shape, F32),
                pltpu.SMEM(cols.shape, I32),
                pltpu.VMEM((months, nb, kk, bs, bs), F32),
                pltpu.VMEM((months, nb, kk * bs, bs), BF16),
                pltpu.VMEM((months, nb, kk * bs, bs), BF16),
                pltpu.VMEM((nbatch, nb, TB, bs), F32),
                pltpu.VMEM((nbatch, nb, TB, bs), F32),
                pltpu.VMEM((nbatch, nb, TB, bs), F32),
                pltpu.VMEM((nb, 2 * TB, bs), BF16),
                pltpu.VMEM((nb, TB, bs), F32),
                pltpu.VMEM((slots, 2 * TB, bs), BF16),
                pltpu.VMEM((nb, TB, bs), F32),
                pltpu.VMEM((nbatch, 3, slots, TB, bs), F32),
                pltpu.VMEM((nbatch, months, slots, TB, bs), F32),
                pltpu.VMEM((nbatch, TB, bs), F32),
                pltpu.VMEM((nbatch, n - 1, TB, bs), F32),
                pltpu.VMEM((nbatch, TB, rows), F32),
                pltpu.VMEM((2, n - 1) + cols.shape, I32),
                pltpu.SMEM((2, n - 1) + cols.shape, I32),
                pltpu.SMEM((3 * slots,), I32),
                pltpu.SMEM((months * nb * FAR,), I32),
                dma((4,)), dma((months, nb)),
                dma, dma, dma,
                dma((nbatch, 3)), dma((nbatch, months)),
                dma((nbatch,)), dma((nbatch,)),
                dma((nbatch,)), dma((nbatch,)),
                dma((nbatch,)), dma,
            ],
            compiler_params=pltpu.CompilerParams(
                collective_id=0, has_side_effects=True, vmem_limit_bytes=63 * 1024 * 1024 + 768 * 1024
            ),
        )(tracers, targets.reshape(1, -1), retain, blocks, cols)

    return jax.shard_map(
        local,
        mesh=mesh,
        in_specs=(
            P(None, "grid"),
            P(),
            P("month", "grid"),
            P("month", "grid", None, None, None),
            P("month", "grid", None),
        ),
        out_specs=P("month", "grid"),
        check_vma=False,
    )
```
